512 devices in a mesh: seq: 64 (over z, y), head: 8 (over x, core).
Axes of the slice: x: 4, y: 4, z: 16, core: 2. Of those that a mesh axis runs over, the one named last changes fastest.
Arguments:
- queries: bfloat16 [16384, 4096], P('seq', 'head'), may hold values from -1.796875 to 1.796875
- key_rows: bfloat16 [16384, 4096], P('seq', 'head'), may hold values from -1.796875 to 1.796875
- values: bfloat16 [16384, 4096], P('seq', 'head'), may hold values from -100 to 100
- out_weight: bfloat16 [4096, 4096], P('head', 'seq'), may hold values from -0.25 to 0.25
- out_grad: bfloat16 [16384, 4096], P('seq', 'head'), may hold values from -6 to 6
Outputs:
- mixed: bfloat16 [16384, 4096], P('seq', 'head')
- query_grad: bfloat16 [16384, 4096], P('seq', 'head')
- key_grad: bfloat16 [16384, 4096], P('seq', 'head')
- value_grad: bfloat16 [16384, 4096], P('seq', 'head')
The draws below stay inside these ranges and needn't reach their ends.
All inputs are finite; a program needn't handle non-finite values.
Results may differ from the reference program's by a relative error of at most 0.014.
Values may be sent and summed in bfloat16 or wider, within the bound.
No kernel may reach another device: no remote copies, remote signals or barrier semaphores. Data moves between devices by JAX's collectives and lax.ppermute only.
A program may use at most 64 MiB of HBM per device.

```python
import math
import jax
import jax.numpy as jnp
from jax import lax

D = 4096
HEADS = 32
HEAD_DIM = 128
TOK_DEV = 256
TOKENS = 16384
INNER = 4096
N_HEAD = 8


def draw_values(key, part):
    row_key = jax.random.fold_in(key, 11)
    col_key = jax.random.fold_in(key, 12)
    entry_key = jax.random.fold_in(key, 13)
    row_scale = jnp.exp(jax.random.uniform(row_key, (TOKENS, 1), jnp.float32) * math.log(10.0))
    col_scale = jnp.exp(jax.random.uniform(col_key, (1, INNER), jnp.float32) * math.log(10.0))
    entries = jnp.clip(jax.random.normal(entry_key, (TOKENS, INNER), jnp.float32), -4.0, 4.0)
    return (entries * row_scale * col_scale / 4.0).astype(jnp.bfloat16)


def with_spikes(drawn, stream_key, source, target, shards_of, factor):
    owner, partner = [(jnp.arange(drawn.shape[axis_at]) // (drawn.shape[axis_at] // shards_of)).reshape([-1 if axis == axis_at else 1 for axis in range(drawn.ndim)]) for axis_at in (source, target)]
    chosen = jax.random.permutation(stream_key, shards_of)[partner]
    strong = (owner == chosen) | (owner == (partner + shards_of // 2) % shards_of)
    return jnp.where(strong, factor * drawn, drawn)


def block_scale(key, dims, split, low, high):
    def one(position, blocks):
        steps = jax.random.uniform(jax.random.fold_in(jax.random.fold_in(key, 6), position), (blocks,), jnp.float32, low / len(split), high / len(split))
        return jnp.repeat(jnp.exp(steps), dims[position] // blocks).reshape((-1,) + (1,) * (len(dims) - position - 1))

    loudness = one(*split[0])
    for cut in split[1:]:
        loudness = loudness * one(*cut)
    return loudness


def gaussian(key, extent, width, reach, shards=(), kind=jnp.bfloat16):
    gain = block_scale(key, extent, shards, -0.22, 0.18) if shards else 1.0
    array = jax.random.normal(key, extent, jnp.float32) * width * gain
    return jnp.minimum(jnp.maximum(array, -reach), reach).astype(kind)


def heavy_noise(rng, dims, width, reach, pieces, heavy, dtype=jnp.bfloat16):
    array = width * jax.random.normal(rng, dims, jnp.float32)
    if pieces:
        array = array * block_scale(rng, dims, pieces, -0.22, 0.18)
    return jnp.clip(with_spikes(array, jax.random.fold_in(rng, 3), *heavy), -reach, reach).astype(dtype)


def setup_inputs(seed: int = 0) -> dict:
    streams_of = jax.random.split(jax.random.key(seed), 6)
    return {
        "queries": gaussian(streams_of[0], (TOKENS, INNER), 0.3, 1.796875, ((0, 64), (1, 8))),
        "key_rows": gaussian(streams_of[1], (TOKENS, INNER), 0.3, 1.796875, ((0, 64), (1, 8))),
        "values": draw_values(jax.random.fold_in(streams_of[5], 71), 0),
        "out_weight": heavy_noise(streams_of[3], (INNER, D), INNER ** -0.5, 0.25, ((0, 8), (1, 64)), (0, 1, 64, 4.0)),
        "out_grad": gaussian(streams_of[4], (TOKENS, D), 1.0, 6.0, ((0, 64), (1, 8))),
    }


def rounded(tensor):
    return lax.optimization_barrier(tensor.astype(jnp.bfloat16)).astype(jnp.float32)

def lower_mask(length):
    row_ids = lax.broadcasted_iota(jnp.int32, (length, length), 0)
    col_ids = lax.broadcasted_iota(jnp.int32, (length, length), 1)
    return row_ids >= col_ids

def reference(queries, key_rows, values, out_weight, out_grad):
    block_count = TOKENS // TOK_DEV
    head_shape = (block_count, TOK_DEV, HEADS, HEAD_DIM)
    query_blocks = queries.reshape(head_shape)
    key_blocks = key_rows.reshape(head_shape)
    value_blocks = values.reshape(head_shape)
    grad_blocks = out_grad.reshape(block_count, TOK_DEV, D)
    causal = lower_mask(TOK_DEV)[None]
    group_width = INNER // N_HEAD

    def state_of(packed):
        key_part, value_part = packed
        return jnp.einsum('shd,she->hde', key_part.astype(jnp.float32), value_part.astype(jnp.float32))
    local_state = lax.map(state_of, (key_blocks, value_blocks))
    running_state = jnp.cumsum(local_state, axis=0)
    prefix_state = jnp.concatenate([jnp.zeros_like(local_state[:1]), running_state[:-1]], axis=0)

    def forward(packed):
        query_part, key_part, value_part, prefix_part, grad_part = packed
        query_wide = query_part.astype(jnp.float32)
        key_wide = key_part.astype(jnp.float32)
        value_wide = value_part.astype(jnp.float32)
        scores = jnp.einsum('thd,shd->hts', query_wide, key_wide)
        weights = rounded(jnp.where(causal, scores, 0.0))
        numerator = jnp.einsum('hts,she->the', weights, value_wide) + jnp.einsum('thd,hde->the', query_wide, rounded(prefix_part))
        spread = jnp.sqrt(lax.optimization_barrier(jnp.mean(numerator * numerator, axis=-1, keepdims=True)) + 1e-06)
        normed = numerator / spread
        attended = normed.astype(jnp.bfloat16).reshape(TOK_DEV, INNER)
        summed = jnp.zeros((TOK_DEV, D), jnp.float32)
        for group in range(N_HEAD):
            first_col = group * group_width
            term = jnp.dot(attended[:, first_col:first_col + group_width], out_weight[first_col:first_col + group_width], preferred_element_type=jnp.float32)
            summed = summed + rounded(term)
        layer_out = summed.astype(jnp.bfloat16)
        out_dir = lax.dot_general(grad_part, out_weight, (((1,), (1,)), ((), ())), preferred_element_type=jnp.float32)
        out_dir = out_dir.reshape(TOK_DEV, HEADS, HEAD_DIM)
        along_dir = lax.optimization_barrier(jnp.mean(out_dir * normed, axis=-1, keepdims=True))
        numer_grad = rounded((out_dir - normed * along_dir) / spread)
        local_grad = jnp.einsum('thd,the->hde', query_wide, numer_grad)
        return (layer_out, numer_grad, local_grad)
    layer_out, numer_grad, local_grad = lax.map(forward, (query_blocks, key_blocks, value_blocks, prefix_state, grad_blocks))
    reversed_sum = jnp.cumsum(local_grad[::-1], axis=0)[::-1]
    suffix_grad = jnp.concatenate([reversed_sum[1:], jnp.zeros_like(local_grad[:1])], axis=0)

    def backward(packed):
        query_part, key_part, value_part, prefix_part, suffix_part, numer_part = packed
        query_wide = query_part.astype(jnp.float32)
        key_wide = key_part.astype(jnp.float32)
        value_wide = value_part.astype(jnp.float32)
        scores = jnp.einsum('thd,shd->hts', query_wide, key_wide)
        weights = rounded(jnp.where(causal, scores, 0.0))
        pair_scores = jnp.einsum('the,she->hts', numer_part, value_wide)
        pair_low = rounded(jnp.where(causal, pair_scores, 0.0))
        prefix_low = rounded(prefix_part)
        suffix_low = rounded(suffix_part)
        query_out = jnp.einsum('hts,shd->thd', pair_low, key_wide) + jnp.einsum('the,hde->thd', numer_part, prefix_low)
        key_out = jnp.einsum('hts,thd->shd', pair_low, query_wide) + jnp.einsum('she,hde->shd', value_wide, suffix_low)
        value_out = jnp.einsum('hts,the->she', weights, numer_part) + jnp.einsum('shd,hde->she', key_wide, suffix_low)
        flat_shape = (TOK_DEV, INNER)
        return (query_out.reshape(flat_shape).astype(jnp.bfloat16), key_out.reshape(flat_shape).astype(jnp.bfloat16), value_out.reshape(flat_shape).astype(jnp.bfloat16))
    query_grad, key_grad, value_grad = lax.map(backward, (query_blocks, key_blocks, value_blocks, prefix_state, suffix_grad, numer_grad))
    return (layer_out.reshape(TOKENS, D), query_grad.reshape(TOKENS, INNER), key_grad.reshape(TOKENS, INNER), value_grad.reshape(TOKENS, INNER))
```

```python
import jax
import jax.numpy as jnp
from jax import lax
from jax.experimental import pallas as pl
from jax.experimental.pallas import tpu as pltpu
from jax.sharding import Mesh, PartitionSpec as P

HEAD_DIM = 128
NEAR = 16
F32 = jnp.float32
BF16 = jnp.bfloat16
AXES = ("zh", "zl", "y", "x", "core")
SIZES = (4, 4, 4, 4, 2)
PARAMS = pltpu.CompilerParams(vmem_limit_bytes=40 * 1024 * 1024)


def dot(left, right, dims):
    return lax.dot_general(left, right, (dims, ((), ())), preferred_element_type=F32)


def shape_of(dims, dtype):
    return jax.ShapeDtypeStruct(dims, dtype)


def call(kernel, out_shape, *operands, smem=0, after=(), name=None):
    count = len(operands)
    spaces = [pltpu.SMEM] * smem + [pltpu.VMEM] * (count - smem) + [pl.ANY] * len(after)
    operands = operands + tuple(after)

    def body(*refs):
        kernel(*refs[:count], *refs[count + len(after) :])

    return pl.pallas_call(
        body,
        out_shape=out_shape,
        in_specs=[pl.BlockSpec(memory_space=s) for s in spaces],
        compiler_params=PARAMS,
        name=name,
    )(*operands)


def head_cols(head):
    return slice(head * HEAD_DIM, (head + 1) * HEAD_DIM)


def causal_mask(length):
    rows = lax.broadcasted_iota(jnp.int32, (length, length), 0)
    cols = lax.broadcasted_iota(jnp.int32, (length, length), 1)
    return rows >= cols


def state_kernel(left_ref, right_ref, out_ref):
    for head in range(left_ref.shape[1] // HEAD_DIM):
        cols = head_cols(head)
        out_ref[cols, :] = dot(left_ref[:, cols], right_ref[:, cols], ((0,), (0,))).astype(BF16)


def near_kernel(reverse, pieces_ref, *refs):
    scan_ref, total_ref = refs[-3:-1] if len(refs) > 2 else refs
    for at, grad_ref in enumerate(refs[:-3]):
        refs[-1][at] = grad_ref[...]
    count = pieces_ref.shape[0]
    running = jnp.zeros(pieces_ref.shape[1:], F32)
    for step in range(count):
        at = count - 1 - step if reverse else step
        scan_ref[at] = running
        running = running + pieces_ref[at].astype(F32)
    total = running.astype(BF16)
    for at in range(total_ref.shape[0]):
        total_ref[at] = total


def far_kernel(reverse, group_ref, scan_ref, totals_ref, out_ref):
    group = group_ref[0]
    offset = jnp.zeros(scan_ref.shape[1:], F32)
    for other in range(totals_ref.shape[0]):
        counts = other > group if reverse else other < group
        offset = offset + jnp.where(counts, totals_ref[other].astype(F32), 0.0)
    for at in range(scan_ref.shape[0]):
        out_ref[at] = (scan_ref[at] + offset).astype(BF16)


def outside_sum(local, group, reverse, grads=()):
    near = ("zl", "y")
    piece = (NEAR, local.shape[0] // NEAR, HEAD_DIM)
    pieces = lax.all_to_all(local.reshape(piece), near, 0, 0, tiled=True)
    stacked = (shape_of((len(grads),) + grads[0].shape, BF16),) if grads else ()
    scan, total, *stack = call(
        lambda *refs: near_kernel(reverse, *refs),
        (shape_of(piece, F32), shape_of((SIZES[0],) + piece[1:], BF16)) + stacked,
        pieces, *grads,
        name="near_scan",
    )
    stack += [permute(own, lambda across, half: (across, 1 - half)) for own in stack]
    totals = lax.all_to_all(total, "zh", 0, 0, tiled=True)
    sums = call(
        lambda *refs: far_kernel(reverse, *refs),
        shape_of(piece, BF16),
        group,
        scan,
        totals,
        smem=1,
        after=stack,
        name="far_scan",
    )
    return lax.all_to_all(sums, near, 0, 0, tiled=True).reshape(local.shape), *stack


def forward_kernel(query_ref, key_ref, value_ref, prefix_ref, numer_ref, attended_ref):
    causal = causal_mask(query_ref.shape[0])
    for head in range(query_ref.shape[1] // HEAD_DIM):
        cols = head_cols(head)
        query = query_ref[:, cols]
        scores = dot(query, key_ref[:, cols], ((1,), (1,)))
        weights = jnp.where(causal, scores, 0.0).astype(BF16)
        numer = dot(weights, value_ref[:, cols], ((1,), (0,)))
        numer = numer + dot(query, prefix_ref[cols, :], ((1,), (0,)))
        spread = jnp.sqrt(jnp.mean(numer * numer, axis=-1, keepdims=True) + 1e-06)
        numer_ref[:, cols] = numer
        attended_ref[:, cols] = (numer / spread).astype(BF16)


def middle_kernel(
    place_ref, own_ref, other_ref, weight_ref, query_ref, numer_ref, numer_grad_ref, local_grad_ref
):
    across, core = place_ref[0], place_ref[1]
    chips, _, width = own_ref.shape
    out_dir = jnp.zeros(numer_ref.shape, F32)
    for ahead in range(chips):
        chip = lax.rem(across + ahead, chips)
        for grad_ref, owner in ((own_ref, core), (other_ref, 1 - core)):
            start = pl.multiple_of((chip * 2 + owner) * width, width)
            out_dir = out_dir + dot(grad_ref[ahead], weight_ref[pl.ds(start, width), :], ((1,), (0,)))
    for head in range(width // HEAD_DIM):
        cols = head_cols(head)
        numer = numer_ref[:, cols]
        spread = jnp.sqrt(jnp.mean(numer * numer, axis=-1, keepdims=True) + 1e-06)
        normed = numer / spread
        here = out_dir[:, cols]
        along = jnp.mean(here * normed, axis=-1, keepdims=True)
        numer_grad = ((here - normed * along) / spread).astype(BF16)
        numer_grad_ref[:, cols] = numer_grad
        local_grad_ref[cols, :] = dot(query_ref[:, cols], numer_grad, ((0,), (0,))).astype(BF16)


def backward_kernel(
    query_ref, key_ref, value_ref, numer_grad_ref, prefix_ref, suffix_ref, query_out, key_out, value_out
):
    causal = causal_mask(query_ref.shape[0])
    for head in range(query_ref.shape[1] // HEAD_DIM):
        cols = head_cols(head)
        query, key, value = query_ref[:, cols], key_ref[:, cols], value_ref[:, cols]
        numer_grad, prefix, suffix = numer_grad_ref[:, cols], prefix_ref[cols, :], suffix_ref[cols, :]
        weights = jnp.where(causal, dot(query, key, ((1,), (1,))), 0.0).astype(BF16)
        pairs = jnp.where(causal, dot(numer_grad, value, ((1,), (1,))), 0.0).astype(BF16)
        query_out[:, cols] = (
            dot(pairs, key, ((1,), (0,))) + dot(numer_grad, prefix, ((1,), (1,)))
        ).astype(BF16)
        key_out[:, cols] = (
            dot(pairs, query, ((0,), (0,))) + dot(value, suffix, ((1,), (1,)))
        ).astype(BF16)
        value_out[:, cols] = (
            dot(weights, numer_grad, ((0,), (0,))) + dot(key, suffix, ((1,), (0,)))
        ).astype(BF16)


def permute(value, move):
    zh, zl, y, x, core = SIZES
    pairs = []
    for seq in range(zh * zl * y):
        for across in range(x):
            for half in range(core):
                to_across, to_half = move(across, half)
                pairs.append(
                    ((seq * x + across) * core + half, (seq * x + to_across % x) * core + to_half)
                )
    return lax.ppermute(value, AXES, pairs)


def per_device(queries, key_rows, values, out_weight, out_grad):
    rows, width = queries.shape
    group = lax.axis_index("zh").astype(jnp.int32).reshape(1)
    place = jnp.stack([lax.axis_index("x"), lax.axis_index("core")]).astype(jnp.int32)

    weight = out_weight.T
    copies = jnp.broadcast_to(weight[None], (SIZES[2],) + weight.shape)
    weight = lax.all_to_all(copies, "y", 0, 0, tiled=True).reshape(-1, width)
    weight = lax.all_gather(weight, ("zh", "zl"), axis=0, tiled=True)

    grads = [out_grad] + [
        permute(out_grad, lambda across, half, ahead=ahead: (across - ahead, half)) for ahead in (1, 2, 3)
    ]

    local_state = call(state_kernel, shape_of((width, HEAD_DIM), BF16), key_rows, values, name="state")
    prefix, own_grads, other_grads = outside_sum(local_state, group, False, grads)
    numer, attended = call(
        forward_kernel,
        (shape_of((rows, width), F32), shape_of((rows, width), BF16)),
        queries, key_rows, values, prefix,
        name="forward",
    )
    numer_grad, local_grad = call(
        middle_kernel,
        (shape_of((rows, width), BF16), shape_of((width, HEAD_DIM), BF16)),
        place, own_grads, other_grads, weight, queries, numer,
        smem=1,
        name="middle",
    )
    partial_out = dot(attended, weight, ((1,), (1,))).astype(BF16)
    mixed = lax.psum_scatter(partial_out, ("x", "core"), scatter_dimension=1, tiled=True)
    (suffix,) = outside_sum(local_grad, group, True)
    query_out, key_out, value_out = call(
        backward_kernel,
        (shape_of((rows, width), BF16),) * 3,
        queries, key_rows, values, numer_grad, prefix, suffix,
        name="backward",
    )
    return mixed, query_out, key_out, value_out


def solution(mesh):
    fine = Mesh(mesh.devices.reshape(SIZES), AXES)
    seq, head = ("zh", "zl", "y"), ("x", "core")
    rows = P(seq, head)
    return jax.shard_map(
        per_device,
        mesh=fine,
        in_specs=(rows, rows, rows, P(head, seq), rows),
        out_specs=(rows, rows, rows, rows),
        check_vma=False,
    )
```

```python
import jax
import jax.numpy as jnp
from jax import lax
from jax.experimental import pallas as pl
from jax.experimental.pallas import tpu as pltpu
from jax.sharding import Mesh, PartitionSpec as P

HEAD_DIM = 128
NEAR = 16
F32 = jnp.float32
BF16 = jnp.bfloat16
AXES = ("zh", "zl", "y", "x", "core")
SIZES = (4, 4, 4, 4, 2)
PARAMS = pltpu.CompilerParams(vmem_limit_bytes=24 * 1024 * 1024)


def dot(left, right, dims):
    return lax.dot_general(left, right, (dims, ((), ())), preferred_element_type=F32)


def shape_of(dims, dtype):
    return jax.ShapeDtypeStruct(dims, dtype)


def call(kernel, out_shape, *operands, smem=0, after=(), name=None):
    count = len(operands)
    spaces = [pltpu.SMEM] * smem + [pltpu.VMEM] * (count - smem) + [pl.ANY] * len(after)
    operands = operands + tuple(after)

    def body(*refs):
        kernel(*refs[:count], *refs[count + len(after) :])

    return pl.pallas_call(
        body,
        out_shape=out_shape,
        in_specs=[pl.BlockSpec(memory_space=s) for s in spaces],
        compiler_params=PARAMS,
        name=name,
    )(*operands)


def head_cols(head):
    return slice(head * HEAD_DIM, (head + 1) * HEAD_DIM)


def causal_mask(length):
    rows = lax.broadcasted_iota(jnp.int32, (length, length), 0)
    cols = lax.broadcasted_iota(jnp.int32, (length, length), 1)
    return rows >= cols


def state_kernel(left_ref, right_ref, out_ref):
    for head in range(left_ref.shape[1] // HEAD_DIM):
        cols = head_cols(head)
        out_ref[cols, :] = dot(left_ref[:, cols], right_ref[:, cols], ((0,), (0,))).astype(BF16)


def near_kernel(reverse, pieces_ref, *refs):
    scan_ref, total_ref = refs[-3:-1] if len(refs) > 2 else refs
    for at, grad_ref in enumerate(refs[:-3]):
        refs[-1][at] = grad_ref[...]
    count = pieces_ref.shape[0]
    running = jnp.zeros(pieces_ref.shape[1:], F32)
    for step in range(count):
        at = count - 1 - step if reverse else step
        scan_ref[at] = running
        running = running + pieces_ref[at].astype(F32)
    total = running.astype(BF16)
    for at in range(total_ref.shape[0]):
        total_ref[at] = total


def far_kernel(reverse, group_ref, scan_ref, totals_ref, out_ref):
    group = group_ref[0]
    offset = jnp.zeros(scan_ref.shape[1:], F32)
    for other in range(totals_ref.shape[0]):
        counts = other > group if reverse else other < group
        offset = offset + jnp.where(counts, totals_ref[other].astype(F32), 0.0)
    for at in range(scan_ref.shape[0]):
        out_ref[at] = (scan_ref[at] + offset).astype(BF16)


def outside_sum(local, group, reverse, grads=()):
    near = ("zl", "y")
    piece = (NEAR, local.shape[0] // NEAR, HEAD_DIM)
    pieces = lax.all_to_all(local.reshape(piece), near, 0, 0, tiled=True)
    stacked = (shape_of((len(grads),) + grads[0].shape, BF16),) if grads else ()
    scan, total, *stack = call(
        lambda *refs: near_kernel(reverse, *refs),
        (shape_of(piece, F32), shape_of((SIZES[0],) + piece[1:], BF16)) + stacked,
        pieces, *grads,
        name="near_scan",
    )
    stack += [permute(own, lambda across, half: (across, 1 - half)) for own in stack]
    totals = lax.all_to_all(total, "zh", 0, 0, tiled=True)
    sums = call(
        lambda *refs: far_kernel(reverse, *refs),
        shape_of(piece, BF16),
        group,
        scan,
        totals,
        smem=1,
        after=stack,
        name="far_scan",
    )
    return lax.all_to_all(sums, near, 0, 0, tiled=True).reshape(local.shape), *stack


def forward_kernel(query_ref, key_ref, value_ref, prefix_ref, numer_ref):
    causal = causal_mask(query_ref.shape[0])
    for head in range(query_ref.shape[1] // HEAD_DIM):
        cols = head_cols(head)
        query = query_ref[:, cols]
        scores = dot(query, key_ref[:, cols], ((1,), (1,)))
        weights = jnp.where(causal, scores, 0.0).astype(BF16)
        numer = dot(weights, value_ref[:, cols], ((1,), (0,)))
        numer = numer + dot(query, prefix_ref[cols, :], ((1,), (0,)))
        numer_ref[:, cols] = numer


def middle_kernel(
    place_ref, own_hbm, other_hbm, weight_hbm, query_ref, numer_ref,
    numer_grad_ref, local_grad_ref, partial_hbm,
    weight_ref, grad_ref, attended_ref, out_dir_ref, partial_ref, in_sems, grad_sems, out_sems,
):
    chips, rows, width = own_hbm.shape
    across, core = place_ref[0], place_ref[1]

    def share(step):
        owner = core if step % 2 == 0 else 1 - core
        start = (lax.rem(across + step // 2, chips) * 2 + owner) * width
        return pl.ds(pl.multiple_of(start, width), width)

    fetches = [
        pltpu.make_async_copy(weight_hbm.at[share(step), :], weight_ref.at[step], in_sems.at[step])
        for step in range(2 * chips)
    ]
    grads = [
        pltpu.make_async_copy(
            (own_hbm if step % 2 == 0 else other_hbm).at[step // 2], grad_ref.at[step], grad_sems.at[step]
        )
        for step in range(2 * chips)
    ]
    for fetch, grad in zip(fetches, grads):
        fetch.start()
        grad.start()
    for head in range(width // HEAD_DIM):
        cols = head_cols(head)
        numer = numer_ref[:, cols]
        spread = jnp.sqrt(jnp.mean(numer * numer, axis=-1, keepdims=True) + 1e-06)
        attended_ref[:, cols] = (numer / spread).astype(BF16)
    sends = []
    for step in range(2 * chips):
        fetches[step].wait()
        grads[step].wait()
        term = dot(grad_ref[step], weight_ref[step], ((1,), (0,)))
        if step == 0:
            out_dir_ref[...] = term
        else:
            out_dir_ref[...] += term
        partial_ref[step] = dot(attended_ref[...], weight_ref[step], ((1,), (1,))).astype(BF16)
        sends.append(
            pltpu.make_async_copy(partial_ref.at[step], partial_hbm.at[:, share(step)], out_sems.at[step])
        )
        sends[step].start()
    for head in range(width // HEAD_DIM):
        cols = head_cols(head)
        numer = numer_ref[:, cols]
        spread = jnp.sqrt(jnp.mean(numer * numer, axis=-1, keepdims=True) + 1e-06)
        normed = numer / spread
        direction = out_dir_ref[:, cols]
        along = jnp.mean(direction * normed, axis=-1, keepdims=True)
        numer_grad = ((direction - normed * along) / spread).astype(BF16)
        numer_grad_ref[:, cols] = numer_grad
        local_grad_ref[cols, :] = dot(query_ref[:, cols], numer_grad, ((0,), (0,))).astype(BF16)
    for send in sends:
        send.wait()


def middle(place, own, other, weight, queries, numer):
    chips, rows, width = own.shape
    shares = 2 * chips
    vmem = pl.BlockSpec(memory_space=pltpu.VMEM)
    hbm = pl.BlockSpec(memory_space=pltpu.HBM)
    return pl.pallas_call(
        middle_kernel,
        out_shape=(
            shape_of((rows, width), BF16),
            shape_of((width, HEAD_DIM), BF16),
            shape_of((rows, shares * width), BF16),
        ),
        in_specs=[pl.BlockSpec(memory_space=pltpu.SMEM), hbm, hbm, hbm, vmem, vmem],
        out_specs=[vmem, vmem, hbm],
        scratch_shapes=[
            pltpu.VMEM((shares, width, width), BF16),
            pltpu.VMEM((shares, rows, width), BF16),
            pltpu.VMEM((rows, width), BF16),
            pltpu.VMEM((rows, width), F32),
            pltpu.VMEM((shares, rows, width), BF16),
            pltpu.SemaphoreType.DMA((shares,)),
            pltpu.SemaphoreType.DMA((shares,)),
            pltpu.SemaphoreType.DMA((shares,)),
        ],
        compiler_params=pltpu.CompilerParams(vmem_limit_bytes=60 * 1024 * 1024),
        name="middle",
    )(place, own, other, weight, queries, numer)


def backward_kernel(
    query_ref, key_ref, value_ref, numer_grad_ref, prefix_ref, query_out, key_part, value_part
):
    causal = causal_mask(query_ref.shape[0])
    for head in range(query_ref.shape[1] // HEAD_DIM):
        cols = head_cols(head)
        query, key, value = query_ref[:, cols], key_ref[:, cols], value_ref[:, cols]
        numer_grad = numer_grad_ref[:, cols]
        weights = jnp.where(causal, dot(query, key, ((1,), (1,))), 0.0).astype(BF16)
        pairs = jnp.where(causal, dot(numer_grad, value, ((1,), (1,))), 0.0).astype(BF16)
        query_out[:, cols] = (
            dot(pairs, key, ((1,), (0,))) + dot(numer_grad, prefix_ref[cols, :], ((1,), (1,)))
        ).astype(BF16)
        key_part[:, cols] = dot(pairs, query, ((0,), (0,)))
        value_part[:, cols] = dot(weights, numer_grad, ((0,), (0,)))


def suffix_kernel(key_ref, value_ref, suffix_ref, key_part, value_part, key_out, value_out):
    for head in range(key_ref.shape[1] // HEAD_DIM):
        cols = head_cols(head)
        suffix = suffix_ref[cols, :]
        key_out[:, cols] = (key_part[:, cols] + dot(value_ref[:, cols], suffix, ((1,), (1,)))).astype(BF16)
        value_out[:, cols] = (value_part[:, cols] + dot(key_ref[:, cols], suffix, ((1,), (0,)))).astype(BF16)


def permute(value, move):
    zh, zl, y, x, core = SIZES
    pairs = []
    for seq in range(zh * zl * y):
        for across in range(x):
            for half in range(core):
                to_across, to_half = move(across, half)
                pairs.append(
                    ((seq * x + across) * core + half, (seq * x + to_across % x) * core + to_half)
                )
    return lax.ppermute(value, AXES, pairs)


def per_device(queries, key_rows, values, out_weight, out_grad):
    rows, width = queries.shape
    group = lax.axis_index("zh").astype(jnp.int32).reshape(1)
    place = jnp.stack([lax.axis_index("x"), lax.axis_index("core")]).astype(jnp.int32)

    weight = out_weight.T
    copies = jnp.broadcast_to(weight[None], (SIZES[2],) + weight.shape)
    weight = lax.all_to_all(copies, "y", 0, 0, tiled=True).reshape(-1, width)
    weight = lax.all_gather(weight, ("zh", "zl"), axis=0, tiled=True)

    grads = [out_grad] + [
        permute(out_grad, lambda across, half, ahead=ahead: (across - ahead, half)) for ahead in (1, 2, 3)
    ]

    local_state = call(state_kernel, shape_of((width, HEAD_DIM), BF16), key_rows, values, name="state")
    prefix, own_grads, other_grads = outside_sum(local_state, group, False, grads)
    numer = call(
        forward_kernel, shape_of((rows, width), F32), queries, key_rows, values, prefix, name="forward"
    )
    numer_grad, local_grad, partial_out = middle(place, own_grads, other_grads, weight, queries, numer)
    mixed = lax.psum_scatter(partial_out, ("x", "core"), scatter_dimension=1, tiled=True)
    (suffix,) = outside_sum(local_grad, group, True)
    query_out, key_part, value_part = call(
        backward_kernel,
        (shape_of((rows, width), BF16),) + (shape_of((rows, width), F32),) * 2,
        queries, key_rows, values, numer_grad, prefix,
        name="backward",
    )
    key_out, value_out = call(
        suffix_kernel,
        (shape_of((rows, width), BF16),) * 2,
        key_rows, values, suffix, key_part, value_part,
        name="suffix",
    )
    return mixed, query_out, key_out, value_out


def solution(mesh):
    fine = Mesh(mesh.devices.reshape(SIZES), AXES)
    seq, head = ("zh", "zl", "y"), ("x", "core")
    rows = P(seq, head)
    return jax.shard_map(
        per_device,
        mesh=fine,
        in_specs=(rows, rows, rows, P(head, seq), rows),
        out_specs=(rows, rows, rows, rows),
        check_vma=False,
    )
```

```python
import jax
import jax.numpy as jnp
from jax import lax
from jax.experimental import pallas as pl
from jax.experimental.pallas import tpu as pltpu
from jax.sharding import Mesh, PartitionSpec as P

HEAD_DIM = 128
NEAR = 16
F32 = jnp.float32
BF16 = jnp.bfloat16
CHUNK = 64
AXES = ("zh", "zl", "y", "x", "core")
SIZES = (4, 4, 4, 4, 2)
PARAMS = pltpu.CompilerParams(vmem_limit_bytes=24 * 1024 * 1024)


def dot(left, right, dims):
    return lax.dot_general(left, right, (dims, ((), ())), preferred_element_type=F32)


def shape_of(dims, dtype):
    return jax.ShapeDtypeStruct(dims, dtype)


def call(kernel, out_shape, *operands, smem=0, after=(), scratch=(), name=None):
    count = len(operands)
    spaces = [pltpu.SMEM] * smem + [pltpu.VMEM] * (count - smem) + [pl.ANY] * len(after)
    operands = operands + tuple(after)

    def body(*refs):
        kernel(*refs[:count], *refs[count + len(after) :])

    return pl.pallas_call(
        body,
        out_shape=out_shape,
        in_specs=[pl.BlockSpec(memory_space=s) for s in spaces],
        scratch_shapes=scratch,
        compiler_params=PARAMS,
        name=name,
    )(*operands)


def head_cols(head):
    return slice(head * HEAD_DIM, (head + 1) * HEAD_DIM)


def causal_mask(length):
    rows = lax.broadcasted_iota(jnp.int32, (length, length), 0)
    cols = lax.broadcasted_iota(jnp.int32, (length, length), 1)
    return rows >= cols


def state_kernel(left_ref, right_ref, out_ref):
    for head in range(left_ref.shape[1] // HEAD_DIM):
        cols = head_cols(head)
        out_ref[cols, :] = dot(left_ref[:, cols], right_ref[:, cols], ((0,), (0,))).astype(BF16)


def near_kernel(reverse, pieces_ref, *refs):
    scan_ref, total_ref = refs[-3:-1] if len(refs) > 2 else refs
    for at, grad_ref in enumerate(refs[:-3]):
        refs[-1][at] = grad_ref[...]
    count = pieces_ref.shape[0]
    running = jnp.zeros(pieces_ref.shape[1:], F32)
    for step in range(count):
        at = count - 1 - step if reverse else step
        scan_ref[at] = running
        running = running + pieces_ref[at].astype(F32)
    total = running.astype(BF16)
    for at in range(total_ref.shape[0]):
        total_ref[at] = total


def far_kernel(reverse, group_ref, scan_ref, totals_ref, out_ref):
    group = group_ref[0]
    offset = jnp.zeros(scan_ref.shape[1:], F32)
    for other in range(totals_ref.shape[0]):
        counts = other > group if reverse else other < group
        offset = offset + jnp.where(counts, totals_ref[other].astype(F32), 0.0)
    for at in range(scan_ref.shape[0]):
        out_ref[at] = (scan_ref[at] + offset).astype(BF16)


def outside_sum(local, group, reverse, grads=(), near_after=None, far_after=None):
    near = ("zl", "y")
    piece = (NEAR, local.shape[0] // NEAR, HEAD_DIM)
    pieces = lax.all_to_all(local.reshape(piece), near, 0, 0, tiled=True)
    stacked = (shape_of((len(grads),) + grads[0].shape, BF16),) if grads else ()
    scan, total, *stack = call(
        lambda *refs: near_kernel(reverse, *refs),
        (shape_of(piece, F32), shape_of((SIZES[0],) + piece[1:], BF16)) + stacked,
        pieces, *grads,
        after=near_after() if near_after else (),
        name="near_scan",
    )
    totals = lax.all_to_all(total, "zh", 0, 0, tiled=True)
    stack += [permute(own, half=1) for own in stack]
    sums = call(
        lambda *refs: far_kernel(reverse, *refs),
        shape_of(piece, BF16),
        group,
        scan,
        totals,
        smem=1,
        after=far_after(*stack) if far_after else (),
        name="far_scan",
    )
    return lax.all_to_all(sums, near, 0, 0, tiled=True).reshape(local.shape), *stack


def pack_kernel(grad_ref, out_ref):
    half = grad_ref.shape[1] // 2
    for y in range(out_ref.shape[0]):
        low = slice(y * CHUNK, (y + 1) * CHUNK)
        high = slice(half + y * CHUNK, half + (y + 1) * CHUNK)
        out_ref[y] = jnp.concatenate([grad_ref[:, low], grad_ref[:, high]], axis=1)


def unpack_kernel(place_ref, part0_ref, part1_ref, part2_ref, part3_ref, out_ref, slots_ref):
    parts = (part0_ref, part1_ref, part2_ref, part3_ref)
    for back, part_ref in enumerate(parts):
        slots_ref[lax.rem(place_ref[2] + 4 - back, 4)] = part_ref[...]
    pieces = [slots_ref[y][:, half * CHUNK : (half + 1) * CHUNK] for half in range(2) for y in range(4)]
    for pair in range(4):
        cols = head_cols(pair)
        out_ref[:, cols] = jnp.concatenate(pieces[2 * pair : 2 * pair + 2], axis=1)


def forward_kernel(query_ref, key_ref, value_ref, prefix_ref, numer_ref, attended_ref):
    causal = causal_mask(query_ref.shape[0])
    for head in range(query_ref.shape[1] // HEAD_DIM):
        cols = head_cols(head)
        query = query_ref[:, cols]
        scores = dot(query, key_ref[:, cols], ((1,), (1,)))
        weights = jnp.where(causal, scores, 0.0).astype(BF16)
        numer = dot(weights, value_ref[:, cols], ((1,), (0,)))
        numer = numer + dot(query, prefix_ref[cols, :], ((1,), (0,)))
        spread = jnp.sqrt(jnp.mean(numer * numer, axis=-1, keepdims=True) + 1e-06)
        numer_ref[:, cols] = numer
        attended_ref[:, cols] = (numer / spread).astype(BF16)


def partial_kernel(
    place_ref, own_hbm, other_hbm, weight0_hbm, ahead1_hbm, back1_hbm, ahead2_hbm, back2_hbm,
    out0_ref, out1_ref, out2_ref, out3_ref, weight_ref, grad_ref, sems,
):
    across, core, y, near = (place_ref[at] for at in range(4))
    rows = out0_ref.shape[0]

    def at_class(ahead):
        return lax.rem(near + ahead, 4)

    def half_of(owner):
        return pl.ds(pl.multiple_of(owner * HEAD_DIM, HEAD_DIM), HEAD_DIM)

    copies = [
        pltpu.make_async_copy(source, target, sems.at[at])
        for at, (source, target) in enumerate((
            (own_hbm, grad_ref.at[:, :, half_of(core)]),
            (other_hbm, grad_ref.at[:, :, half_of(1 - core)]),
            (weight0_hbm, weight_ref.at[:, at_class(0)]),
            (ahead1_hbm, weight_ref.at[:, at_class(1)]),
            (back1_hbm, weight_ref.at[:, at_class(3)]),
            (ahead2_hbm, weight_ref.at[pl.ds(0, 2), at_class(2)]),
            (back2_hbm, weight_ref.at[pl.ds(2, 2), at_class(2)]),
        ))
    ]
    for copy in copies:
        copy.start()
    for copy in copies:
        copy.wait()
    weights = [weight_ref[lax.rem(across + ahead, 4)].reshape(4 * CHUNK, -1) for ahead in range(4)]
    for block, out_ref in enumerate((out0_ref, out1_ref, out2_ref, out3_ref)):
        tokens = pl.ds(pl.multiple_of(lax.rem(y + block, 4) * rows, rows), rows)
        total = dot(grad_ref[0, tokens, :], weights[0], ((1,), (0,)))
        for ahead in range(1, 4):
            total = total + dot(grad_ref[ahead, tokens, :], weights[ahead], ((1,), (0,)))
        out_ref[...] = total


def partial_out_grad(place, own, other, weights, rows):
    width = weights[0].shape[-1]
    vmem = pl.BlockSpec(memory_space=pltpu.VMEM)
    hbm = pl.BlockSpec(memory_space=pl.ANY)
    return pl.pallas_call(
        partial_kernel,
        out_shape=(shape_of((rows, width), F32),) * 4 + (shape_of((4, 4, CHUNK, width), BF16),),
        in_specs=[pl.BlockSpec(memory_space=pltpu.SMEM)] + [hbm] * 7,
        out_specs=[vmem] * 5,
        scratch_shapes=[pltpu.VMEM((4, 4 * rows, 2 * HEAD_DIM), BF16), pltpu.SemaphoreType.DMA((7,))],
        compiler_params=PARAMS,
        name="partial",
    )(place, own, other, *weights)


def middle_kernel(part0_ref, part1_ref, part2_ref, part3_ref, query_ref, numer_ref, numer_grad_ref, local_grad_ref):
    for head in range(query_ref.shape[1] // HEAD_DIM):
        cols = head_cols(head)
        numer = numer_ref[:, cols]
        spread = jnp.sqrt(jnp.mean(numer * numer, axis=-1, keepdims=True) + 1e-06)
        normed = numer / spread
        direction = part0_ref[:, cols] + part1_ref[:, cols] + part2_ref[:, cols] + part3_ref[:, cols]
        along = jnp.mean(direction * normed, axis=-1, keepdims=True)
        numer_grad = ((direction - normed * along) / spread).astype(BF16)
        numer_grad_ref[:, cols] = numer_grad
        local_grad_ref[cols, :] = dot(query_ref[:, cols], numer_grad, ((0,), (0,))).astype(BF16)


def mixed_kernel(place_ref, att0_ref, att1_ref, att2_ref, att3_ref, weight_ref, own_ref, other_ref):
    across, core, y = (place_ref[at] for at in range(3))
    for chip in range(4):
        weight = weight_ref[lax.rem(across + chip, 4)].reshape(4 * CHUNK, -1)
        for ahead, att_ref in enumerate((att0_ref, att1_ref, att2_ref, att3_ref)):
            block = dot(att_ref[...], weight, ((1,), (1,)))
            low, high = block[:, :HEAD_DIM], block[:, HEAD_DIM:]
            at = lax.rem(y + ahead, 4)
            own_ref[chip, at] = jnp.where(core == 0, low, high).astype(BF16)
            other_ref[chip, at] = jnp.where(core == 0, high, low).astype(BF16)


def core_sum_kernel(own_ref, other_ref, *out_refs):
    for chip, out_ref in enumerate(out_refs):
        for y in range(out_ref.shape[0]):
            out_ref[y] = (own_ref[chip, y].astype(F32) + other_ref[chip, y].astype(F32)).astype(BF16)


def chip_sum_kernel(place_ref, sum0_ref, sum1_ref, sum2_ref, sum3_ref, *out_refs):
    for ahead, out_ref in enumerate(out_refs):
        at = lax.rem(place_ref[2] + ahead, 4)
        total = sum0_ref[at].astype(F32) + sum1_ref[at].astype(F32)
        out_ref[...] = (total + sum2_ref[at].astype(F32) + sum3_ref[at].astype(F32)).astype(BF16)


def backward_kernel(
    query_ref, key_ref, value_ref, numer_grad_ref, prefix_ref, query_out, key_part, value_part
):
    causal = causal_mask(query_ref.shape[0])
    for head in range(query_ref.shape[1] // HEAD_DIM):
        cols = head_cols(head)
        query, key, value = query_ref[:, cols], key_ref[:, cols], value_ref[:, cols]
        numer_grad = numer_grad_ref[:, cols]
        weights = jnp.where(causal, dot(query, key, ((1,), (1,))), 0.0).astype(BF16)
        pairs = jnp.where(causal, dot(numer_grad, value, ((1,), (1,))), 0.0).astype(BF16)
        query_out[:, cols] = (
            dot(pairs, key, ((1,), (0,))) + dot(numer_grad, prefix_ref[cols, :], ((1,), (1,)))
        ).astype(BF16)
        key_part[:, cols] = dot(pairs, query, ((0,), (0,)))
        value_part[:, cols] = dot(weights, numer_grad, ((0,), (0,)))


def suffix_kernel(key_ref, value_ref, suffix_ref, key_part, value_part, key_out, value_out):
    for head in range(key_ref.shape[1] // HEAD_DIM):
        cols = head_cols(head)
        suffix = suffix_ref[cols, :]
        key_out[:, cols] = (key_part[:, cols] + dot(value_ref[:, cols], suffix, ((1,), (1,)))).astype(BF16)
        value_out[:, cols] = (value_part[:, cols] + dot(key_ref[:, cols], suffix, ((1,), (0,)))).astype(BF16)


def permute(value, z=0, y=0, x=0, half=0):
    along_zh, along_zl, along_y, along_x, cores = SIZES
    along_z = along_zh * along_zl

    def number(at_z, at_y, at_x, at_core):
        return (((at_z % along_z) * along_y + at_y % along_y) * along_x + at_x % along_x) * cores + at_core

    pairs = [
        (number(at_z + z, at_y + y, at_x + x, at_core ^ half), number(at_z, at_y, at_x, at_core))
        for at_z in range(along_z)
        for at_y in range(along_y)
        for at_x in range(along_x)
        for at_core in range(cores)
    ]
    return lax.ppermute(value, AXES, pairs)


def per_device(queries, key_rows, values, out_weight, out_grad):
    rows, width = queries.shape
    group = lax.axis_index("zh").astype(jnp.int32).reshape(1)
    place = jnp.stack([lax.axis_index(name) for name in ("x", "core", "y", "zl")]).astype(jnp.int32)

    weight = out_weight.T
    copies = jnp.broadcast_to(weight[None], (SIZES[0],) + weight.shape)
    weight = lax.all_to_all(copies, "zh", 0, 0, tiled=True)
    weights = (
        weight, permute(weight, z=1), permute(weight, z=-1), permute(weight[:2], z=2), permute(weight[2:], z=-2)
    )

    packed = call(pack_kernel, shape_of((SIZES[2], rows, HEAD_DIM), BF16), out_grad, name="pack")
    grad = lax.all_to_all(packed, "y", 0, 0, tiled=True).reshape(SIZES[2] * rows, HEAD_DIM)
    grads = [grad] + [permute(grad, x=ahead) for ahead in (1, 2, 3)]

    local_state = call(
        state_kernel, shape_of((width, HEAD_DIM), BF16), key_rows, values, after=(weight, *grads[1:]), name="state"
    )
    parts = []

    def start_parts(own, other):
        parts.extend(partial_out_grad(place, own, other, weights, rows))
        return parts[-1:]

    prefix, *_ = outside_sum(local_state, group, False, grads, lambda: weights[1:], start_parts)
    *parts, weight = parts
    parts = [parts[0]] + [permute(parts[ahead], y=-ahead) for ahead in (1, 2, 3)]
    numer, attended = call(
        forward_kernel,
        (shape_of((rows, width), F32), shape_of((rows, width), BF16)),
        queries, key_rows, values, prefix,
        after=parts,
        name="forward",
    )
    blocks = [attended] + [permute(attended, y=ahead) for ahead in (1, 2, 3)]
    numer_grad, local_grad = call(
        middle_kernel,
        (shape_of((rows, width), BF16), shape_of((width, HEAD_DIM), BF16)),
        *parts, queries, numer,
        name="middle",
    )

    shares = shape_of((4, 4, rows, HEAD_DIM), BF16)
    own, other = call(mixed_kernel, (shares, shares), place, *blocks, weight, smem=1, after=(local_grad,), name="mixed")
    other = permute(other, half=1)
    sums = call(core_sum_kernel, (shape_of((4, rows, HEAD_DIM), BF16),) * 4, own, other, name="core_sum")
    sums = [sums[0]] + [permute(sums[ahead], x=-ahead) for ahead in (1, 2, 3)]
    tokens = call(
        chip_sum_kernel, (shape_of((rows, HEAD_DIM), BF16),) * 4, place, *sums, smem=1, name="chip_sum"
    )
    tokens = [tokens[0]] + [permute(tokens[ahead], y=-ahead) for ahead in (1, 2, 3)]
    mixed = call(
        unpack_kernel,
        shape_of((rows, width), BF16),
        place, *tokens,
        smem=1,
        scratch=[pltpu.VMEM((4, rows, HEAD_DIM), BF16)],
        name="unpack",
    )

    (suffix,) = outside_sum(
        local_grad, group, True, near_after=lambda: (other,), far_after=lambda: tuple(sums[1:])
    )
    query_out, key_part, value_part = call(
        backward_kernel,
        (shape_of((rows, width), BF16),) + (shape_of((rows, width), F32),) * 2,
        queries, key_rows, values, numer_grad, prefix,
        name="backward",
    )
    key_out, value_out = call(
        suffix_kernel,
        (shape_of((rows, width), BF16),) * 2,
        key_rows, values, suffix, key_part, value_part,
        name="suffix",
    )
    return mixed, query_out, key_out, value_out


def solution(mesh):
    fine = Mesh(mesh.devices.reshape(SIZES), AXES)
    seq, head = ("zh", "zl", "y"), ("x", "core")
    rows = P(seq, head)
    return jax.shard_map(
        per_device,
        mesh=fine,
        in_specs=(rows, rows, rows, P(head, seq), rows),
        out_specs=(rows, rows, rows, rows),
        check_vma=False,
    )
```

```python
import math

import jax
import jax.numpy as jnp
from jax import lax
from jax.experimental import pallas as pl
from jax.experimental.pallas import tpu as pltpu
from jax.sharding import Mesh, PartitionSpec as P

HEAD_DIM = 128
F32 = jnp.float32
BF16 = jnp.bfloat16
AXES = ("zh", "zm", "zl", "y", "x", "core")
SIZES = (4, 2, 2, 4, 4, 2)
SEQ = AXES[:4]
PARAMS = pltpu.CompilerParams(vmem_limit_bytes=24 * 1024 * 1024)


def dot(left, right, dims):
    return lax.dot_general(left, right, (dims, ((), ())), preferred_element_type=F32)


def shape_of(dims, dtype):
    return jax.ShapeDtypeStruct(dims, dtype)


def call(kernel, out_shape, *operands, smem=0, after=(), name=None):
    count = len(operands)
    spaces = [pltpu.SMEM] * smem + [pltpu.VMEM] * (count - smem) + [pl.ANY] * len(after)
    operands = operands + tuple(after)

    def body(*refs):
        kernel(*refs[:count], *refs[count + len(after) :])

    return pl.pallas_call(
        body,
        out_shape=out_shape,
        in_specs=[pl.BlockSpec(memory_space=s) for s in spaces],
        compiler_params=PARAMS,
        name=name,
    )(*operands)


def head_cols(head):
    return slice(head * HEAD_DIM, (head + 1) * HEAD_DIM)


def causal_mask(length):
    rows = lax.broadcasted_iota(jnp.int32, (length, length), 0)
    cols = lax.broadcasted_iota(jnp.int32, (length, length), 1)
    return rows >= cols


def state_kernel(left_ref, right_ref, out_ref):
    for head in range(left_ref.shape[1] // HEAD_DIM):
        cols = head_cols(head)
        out_ref[cols, :] = dot(left_ref[:, cols], right_ref[:, cols], ((0,), (0,))).astype(BF16)


def near_kernel(reverse, pieces_ref, *refs):
    scan_ref, total_ref = refs[-3:-1] if len(refs) > 2 else refs
    for at, grad_ref in enumerate(refs[:-3]):
        refs[-1][at] = grad_ref[...]
    count = pieces_ref.shape[0]
    running = jnp.zeros(pieces_ref.shape[1:], F32)
    for step in range(count):
        at = count - 1 - step if reverse else step
        scan_ref[at] = running
        running = running + pieces_ref[at].astype(F32)
    total = running.astype(BF16)
    for at in range(total_ref.shape[0]):
        total_ref[at] = total


def far_kernel(reverse, split, place_ref, scan_ref, totals_ref, out_ref):
    group = place_ref[1 + split]
    offset = jnp.zeros(scan_ref.shape[1:], F32)
    for other in range(totals_ref.shape[0]):
        counts = other > group if reverse else other < group
        offset = offset + jnp.where(counts, totals_ref[other].astype(F32), 0.0)
    for at in range(scan_ref.shape[0]):
        out_ref[at] = (scan_ref[at] + offset).astype(BF16)


def outside_sum(local, split, reverse, place, grads=()):
    far, near = SEQ[:split], SEQ[split:]
    blocks = lax.axis_size(near)
    piece = (blocks, local.shape[0] // blocks, HEAD_DIM)
    pieces = lax.all_to_all(local.reshape(piece), near, 0, 0, tiled=True)
    stacked = (shape_of((len(grads),) + grads[0].shape, BF16),) if grads else ()
    scan, total, *stack = call(
        lambda *refs: near_kernel(reverse, *refs),
        (shape_of(piece, F32), shape_of((lax.axis_size(far),) + piece[1:], BF16)) + stacked,
        pieces, *grads,
        name="near_scan",
    )
    stack += [permute(own, lambda across, half: (across, 1 - half)) for own in stack]
    totals = lax.all_to_all(total, far, 0, 0, tiled=True)
    sums = call(
        lambda *refs: far_kernel(reverse, split, *refs),
        shape_of(piece, BF16),
        place,
        scan,
        totals,
        smem=1,
        after=stack,
        name="far_scan",
    )
    return lax.all_to_all(sums, near, 0, 0, tiled=True).reshape(local.shape), *stack


def forward_kernel(query_ref, key_ref, value_ref, prefix_ref, numer_ref):
    causal = causal_mask(query_ref.shape[0])
    for head in range(query_ref.shape[1] // HEAD_DIM):
        cols = head_cols(head)
        query = query_ref[:, cols]
        scores = dot(query, key_ref[:, cols], ((1,), (1,)))
        weights = jnp.where(causal, scores, 0.0).astype(BF16)
        numer = dot(weights, value_ref[:, cols], ((1,), (0,)))
        numer = numer + dot(query, prefix_ref[cols, :], ((1,), (0,)))
        numer_ref[:, cols] = numer


def middle_kernel(
    place_ref, own_ref, other_ref, weight_hbm, query_ref, numer_ref,
    numer_grad_ref, local_grad_ref, partial_hbm,
    weight_ref, attended_ref, out_dir_ref, partial_ref, in_sems, out_sems,
):
    chips, rows, width = own_ref.shape
    across, core = place_ref[0], place_ref[1]

    def share(step):
        owner = core if step % 2 == 0 else 1 - core
        start = (lax.rem(across + step // 2, chips) * 2 + owner) * width
        return pl.ds(pl.multiple_of(start, width), width)

    fetches = [
        pltpu.make_async_copy(weight_hbm.at[share(step), :], weight_ref.at[step], in_sems.at[step])
        for step in range(2 * chips)
    ]
    for fetch in fetches:
        fetch.start()
    for head in range(width // HEAD_DIM):
        cols = head_cols(head)
        numer = numer_ref[:, cols]
        spread = jnp.sqrt(jnp.mean(numer * numer, axis=-1, keepdims=True) + 1e-06)
        attended_ref[:, cols] = (numer / spread).astype(BF16)
    sends = []
    for step in range(2 * chips):
        fetches[step].wait()
        grad_ref = own_ref if step % 2 == 0 else other_ref
        term = dot(grad_ref[step // 2], weight_ref[step], ((1,), (0,)))
        if step == 0:
            out_dir_ref[...] = term
        else:
            out_dir_ref[...] += term
        partial_ref[step] = dot(attended_ref[...], weight_ref[step], ((1,), (1,))).astype(BF16)
        sends.append(
            pltpu.make_async_copy(partial_ref.at[step], partial_hbm.at[:, share(step)], out_sems.at[step])
        )
        sends[step].start()
    for head in range(width // HEAD_DIM):
        cols = head_cols(head)
        numer = numer_ref[:, cols]
        spread = jnp.sqrt(jnp.mean(numer * numer, axis=-1, keepdims=True) + 1e-06)
        normed = numer / spread
        direction = out_dir_ref[:, cols]
        along = jnp.mean(direction * normed, axis=-1, keepdims=True)
        numer_grad = ((direction - normed * along) / spread).astype(BF16)
        numer_grad_ref[:, cols] = numer_grad
        local_grad_ref[cols, :] = dot(query_ref[:, cols], numer_grad, ((0,), (0,))).astype(BF16)
    for send in sends:
        send.wait()


def middle(place, own, other, weight, queries, numer):
    chips, rows, width = own.shape
    shares = 2 * chips
    vmem = pl.BlockSpec(memory_space=pltpu.VMEM)
    hbm = pl.BlockSpec(memory_space=pltpu.HBM)
    return pl.pallas_call(
        middle_kernel,
        out_shape=(
            shape_of((rows, width), BF16),
            shape_of((width, HEAD_DIM), BF16),
            shape_of((rows, shares * width), BF16),
        ),
        in_specs=[pl.BlockSpec(memory_space=pltpu.SMEM), vmem, vmem, hbm, vmem, vmem],
        out_specs=[vmem, vmem, hbm],
        scratch_shapes=[
            pltpu.VMEM((shares, width, width), BF16),
            pltpu.VMEM((rows, width), BF16),
            pltpu.VMEM((rows, width), F32),
            pltpu.VMEM((shares, rows, width), BF16),
            pltpu.SemaphoreType.DMA((shares,)),
            pltpu.SemaphoreType.DMA((shares,)),
        ],
        compiler_params=pltpu.CompilerParams(vmem_limit_bytes=50 * 1024 * 1024),
        name="middle",
    )(place, own, other, weight, queries, numer)


def backward_kernel(
    query_ref, key_ref, value_ref, numer_grad_ref, prefix_ref, query_out, key_part, value_part
):
    causal = causal_mask(query_ref.shape[0])
    for head in range(query_ref.shape[1] // HEAD_DIM):
        cols = head_cols(head)
        query, key, value = query_ref[:, cols], key_ref[:, cols], value_ref[:, cols]
        numer_grad = numer_grad_ref[:, cols]
        weights = jnp.where(causal, dot(query, key, ((1,), (1,))), 0.0).astype(BF16)
        pairs = jnp.where(causal, dot(numer_grad, value, ((1,), (1,))), 0.0).astype(BF16)
        query_out[:, cols] = (
            dot(pairs, key, ((1,), (0,))) + dot(numer_grad, prefix_ref[cols, :], ((1,), (1,)))
        ).astype(BF16)
        key_part[:, cols] = dot(pairs, query, ((0,), (0,)))
        value_part[:, cols] = dot(weights, numer_grad, ((0,), (0,)))


def suffix_kernel(key_ref, value_ref, suffix_ref, key_part, value_part, key_out, value_out):
    for head in range(key_ref.shape[1] // HEAD_DIM):
        cols = head_cols(head)
        suffix = suffix_ref[cols, :]
        key_out[:, cols] = (key_part[:, cols] + dot(value_ref[:, cols], suffix, ((1,), (1,)))).astype(BF16)
        value_out[:, cols] = (value_part[:, cols] + dot(key_ref[:, cols], suffix, ((1,), (0,)))).astype(BF16)


def permute(value, move):
    *seqs, x, core = SIZES
    pairs = []
    for seq in range(math.prod(seqs)):
        for across in range(x):
            for half in range(core):
                to_across, to_half = move(across, half)
                pairs.append(
                    ((seq * x + across) * core + half, (seq * x + to_across % x) * core + to_half)
                )
    return lax.ppermute(value, AXES, pairs)


def per_device(queries, key_rows, values, out_weight, out_grad):
    rows, width = queries.shape
    place = [lax.axis_index(axes) for axes in ("x", "core", SEQ[:1], SEQ[:2])]
    place = jnp.stack(place).astype(jnp.int32)

    weight = out_weight.T
    copies = jnp.broadcast_to(weight[None], (SIZES[3],) + weight.shape)
    weight = lax.all_to_all(copies, "y", 0, 0, tiled=True).reshape(-1, width)
    weight = lax.all_gather(weight, SEQ[:3], axis=0, tiled=True)

    grads = [out_grad] + [
        permute(out_grad, lambda across, half, ahead=ahead: (across - ahead, half)) for ahead in (1, 2, 3)
    ]

    local_state = call(state_kernel, shape_of((width, HEAD_DIM), BF16), key_rows, values, name="state")
    prefix, own_grads, other_grads = outside_sum(local_state, 1, False, place, grads)
    numer = call(
        forward_kernel, shape_of((rows, width), F32), queries, key_rows, values, prefix, name="forward"
    )
    numer_grad, local_grad, partial_out = middle(place, own_grads, other_grads, weight, queries, numer)
    mixed = lax.psum_scatter(partial_out, ("x", "core"), scatter_dimension=1, tiled=True)
    (suffix,) = outside_sum(local_grad, 2, True, place)
    query_out, key_part, value_part = call(
        backward_kernel,
        (shape_of((rows, width), BF16),) + (shape_of((rows, width), F32),) * 2,
        queries, key_rows, values, numer_grad, prefix,
        name="backward",
    )
    key_out, value_out = call(
        suffix_kernel,
        (shape_of((rows, width), BF16),) * 2,
        key_rows, values, suffix, key_part, value_part,
        name="suffix",
    )
    return mixed, query_out, key_out, value_out


def solution(mesh):
    fine = Mesh(mesh.devices.reshape(SIZES), AXES)
    head = AXES[4:]
    rows = P(SEQ, head)
    return jax.shard_map(
        per_device,
        mesh=fine,
        in_specs=(rows, rows, rows, P(head, SEQ), rows),
        out_specs=(rows, rows, rows, rows),
        check_vma=False,
    )
```

```python
import math

import jax
import jax.numpy as jnp
from jax import lax
from jax.experimental import pallas as pl
from jax.experimental.pallas import tpu as pltpu
from jax.sharding import Mesh, PartitionSpec as P

HEAD_DIM = 128
F32 = jnp.float32
BF16 = jnp.bfloat16
AXES = ("zh", "zm", "zl", "y", "x", "core")
SIZES = (4, 2, 2, 4, 4, 2)
SEQ = AXES[:4]
PARAMS = pltpu.CompilerParams(vmem_limit_bytes=24 * 1024 * 1024)


def dot(left, right, dims):
    return lax.dot_general(left, right, (dims, ((), ())), preferred_element_type=F32)


def shape_of(dims, dtype):
    return jax.ShapeDtypeStruct(dims, dtype)


def call(kernel, out_shape, *operands, smem=0, after=(), name=None):
    count = len(operands)
    spaces = [pltpu.SMEM] * smem + [pltpu.VMEM] * (count - smem) + [pl.ANY] * len(after)
    operands = operands + tuple(after)

    def body(*refs):
        kernel(*refs[:count], *refs[count + len(after) :])

    return pl.pallas_call(
        body,
        out_shape=out_shape,
        in_specs=[pl.BlockSpec(memory_space=s) for s in spaces],
        compiler_params=PARAMS,
        name=name,
    )(*operands)


def head_cols(head):
    return slice(head * HEAD_DIM, (head + 1) * HEAD_DIM)


def causal_mask(length):
    rows = lax.broadcasted_iota(jnp.int32, (length, length), 0)
    cols = lax.broadcasted_iota(jnp.int32, (length, length), 1)
    return rows >= cols


def state_kernel(left_ref, right_ref, out_ref):
    for head in range(left_ref.shape[1] // HEAD_DIM):
        cols = head_cols(head)
        out_ref[cols, :] = dot(left_ref[:, cols], right_ref[:, cols], ((0,), (0,))).astype(BF16)


def near_kernel(reverse, pieces_ref, *refs):
    scan_ref, total_ref = refs[-3:-1] if len(refs) > 2 else refs
    for at, grad_ref in enumerate(refs[:-3]):
        refs[-1][at] = grad_ref[...]
    count = pieces_ref.shape[0]
    running = jnp.zeros(pieces_ref.shape[1:], F32)
    for step in range(count):
        at = count - 1 - step if reverse else step
        scan_ref[at] = running
        running = running + pieces_ref[at].astype(F32)
    total = running.astype(BF16)
    for at in range(total_ref.shape[0]):
        total_ref[at] = total


def far_kernel(reverse, split, place_ref, scan_ref, totals_ref, out_ref):
    group = place_ref[1 + split]
    offset = jnp.zeros(scan_ref.shape[1:], F32)
    for other in range(totals_ref.shape[0]):
        counts = other > group if reverse else other < group
        offset = offset + jnp.where(counts, totals_ref[other].astype(F32), 0.0)
    for at in range(scan_ref.shape[0]):
        out_ref[at] = (scan_ref[at] + offset).astype(BF16)


def outside_sum(local, split, reverse, place, grads=(), before_far=()):
    far, near = SEQ[:split], SEQ[split:]
    blocks = lax.axis_size(near)
    piece = (blocks, local.shape[0] // blocks, HEAD_DIM)
    pieces = lax.all_to_all(local.reshape(piece), near, 0, 0, tiled=True)
    stacked = (shape_of((len(grads),) + grads[0].shape, BF16),) if grads else ()
    scan, total, *stack = call(
        lambda *refs: near_kernel(reverse, *refs),
        (shape_of(piece, F32), shape_of((lax.axis_size(far),) + piece[1:], BF16)) + stacked,
        pieces, *grads,
        name="near_scan",
    )
    stack += [permute(own, lambda across, half: (across, 1 - half)) for own in stack]
    totals = lax.all_to_all(total, far, 0, 0, tiled=True)
    sums = call(
        lambda *refs: far_kernel(reverse, split, *refs),
        shape_of(piece, BF16),
        place,
        scan,
        totals,
        smem=1,
        after=(*stack, *before_far),
        name="far_scan",
    )
    return lax.all_to_all(sums, near, 0, 0, tiled=True).reshape(local.shape), *stack


def forward_kernel(query_ref, key_ref, value_ref, prefix_ref, numer_ref):
    causal = causal_mask(query_ref.shape[0])
    for head in range(query_ref.shape[1] // HEAD_DIM):
        cols = head_cols(head)
        query = query_ref[:, cols]
        scores = dot(query, key_ref[:, cols], ((1,), (1,)))
        weights = jnp.where(causal, scores, 0.0).astype(BF16)
        numer = dot(weights, value_ref[:, cols], ((1,), (0,)))
        numer = numer + dot(query, prefix_ref[cols, :], ((1,), (0,)))
        numer_ref[:, cols] = numer


def middle_kernel(
    place_ref, own_ref, other_ref, weight_hbm, query_ref, numer_ref,
    numer_grad_ref, local_grad_ref, partial_hbm,
    weight_ref, attended_ref, out_dir_ref, partial_ref, in_sems, out_sems,
):
    chips, rows, width = own_ref.shape
    across, core = place_ref[0], place_ref[1]

    def share(step):
        owner = core if step % 2 == 0 else 1 - core
        start = (lax.rem(across + step // 2, chips) * 2 + owner) * width
        return pl.ds(pl.multiple_of(start, width), width)

    fetches = [
        pltpu.make_async_copy(weight_hbm.at[share(step), :], weight_ref.at[step], in_sems.at[step])
        for step in range(2 * chips)
    ]
    for fetch in fetches:
        fetch.start()
    for head in range(width // HEAD_DIM):
        cols = head_cols(head)
        numer = numer_ref[:, cols]
        spread = jnp.sqrt(jnp.mean(numer * numer, axis=-1, keepdims=True) + 1e-06)
        attended_ref[:, cols] = (numer / spread).astype(BF16)
    sends = []
    for step in range(2 * chips):
        fetches[step].wait()
        grad_ref = own_ref if step % 2 == 0 else other_ref
        term = dot(grad_ref[step // 2], weight_ref[step], ((1,), (0,)))
        if step == 0:
            out_dir_ref[...] = term
        else:
            out_dir_ref[...] += term
        partial_ref[step] = dot(attended_ref[...], weight_ref[step], ((1,), (1,))).astype(BF16)
        sends.append(
            pltpu.make_async_copy(partial_ref.at[step], partial_hbm.at[:, share(step)], out_sems.at[step])
        )
        sends[step].start()
    for head in range(width // HEAD_DIM):
        cols = head_cols(head)
        numer = numer_ref[:, cols]
        spread = jnp.sqrt(jnp.mean(numer * numer, axis=-1, keepdims=True) + 1e-06)
        normed = numer / spread
        direction = out_dir_ref[:, cols]
        along = jnp.mean(direction * normed, axis=-1, keepdims=True)
        numer_grad = ((direction - normed * along) / spread).astype(BF16)
        numer_grad_ref[:, cols] = numer_grad
        local_grad_ref[cols, :] = dot(query_ref[:, cols], numer_grad, ((0,), (0,))).astype(BF16)
    for send in sends:
        send.wait()


def middle(place, own, other, weight, queries, numer):
    chips, rows, width = own.shape
    shares = 2 * chips
    vmem = pl.BlockSpec(memory_space=pltpu.VMEM)
    hbm = pl.BlockSpec(memory_space=pltpu.HBM)
    return pl.pallas_call(
        middle_kernel,
        out_shape=(
            shape_of((rows, width), BF16),
            shape_of((width, HEAD_DIM), BF16),
            shape_of((rows, shares * width), BF16),
        ),
        in_specs=[pl.BlockSpec(memory_space=pltpu.SMEM), vmem, vmem, hbm, vmem, vmem],
        out_specs=[vmem, vmem, hbm],
        scratch_shapes=[
            pltpu.VMEM((shares, width, width), BF16),
            pltpu.VMEM((rows, width), BF16),
            pltpu.VMEM((rows, width), F32),
            pltpu.VMEM((shares, rows, width), BF16),
            pltpu.SemaphoreType.DMA((shares,)),
            pltpu.SemaphoreType.DMA((shares,)),
        ],
        compiler_params=pltpu.CompilerParams(vmem_limit_bytes=50 * 1024 * 1024),
        name="middle",
    )(place, own, other, weight, queries, numer)


def backward_kernel(
    query_ref, key_ref, value_ref, numer_grad_ref, prefix_ref, query_out, key_part, value_part
):
    causal = causal_mask(query_ref.shape[0])
    for head in range(query_ref.shape[1] // HEAD_DIM):
        cols = head_cols(head)
        query, key, value = query_ref[:, cols], key_ref[:, cols], value_ref[:, cols]
        numer_grad = numer_grad_ref[:, cols]
        weights = jnp.where(causal, dot(query, key, ((1,), (1,))), 0.0).astype(BF16)
        pairs = jnp.where(causal, dot(numer_grad, value, ((1,), (1,))), 0.0).astype(BF16)
        query_out[:, cols] = (
            dot(pairs, key, ((1,), (0,))) + dot(numer_grad, prefix_ref[cols, :], ((1,), (1,)))
        ).astype(BF16)
        key_part[:, cols] = dot(pairs, query, ((0,), (0,)))
        value_part[:, cols] = dot(weights, numer_grad, ((0,), (0,)))


def suffix_kernel(key_ref, value_ref, suffix_ref, key_part, value_part, key_out, value_out):
    for head in range(key_ref.shape[1] // HEAD_DIM):
        cols = head_cols(head)
        suffix = suffix_ref[cols, :]
        key_out[:, cols] = (key_part[:, cols] + dot(value_ref[:, cols], suffix, ((1,), (1,)))).astype(BF16)
        value_out[:, cols] = (value_part[:, cols] + dot(key_ref[:, cols], suffix, ((1,), (0,)))).astype(BF16)


def permute(value, move):
    *seqs, x, core = SIZES
    pairs = []
    for seq in range(math.prod(seqs)):
        for across in range(x):
            for half in range(core):
                to_across, to_half = move(across, half)
                pairs.append(
                    ((seq * x + across) * core + half, (seq * x + to_across % x) * core + to_half)
                )
    return lax.ppermute(value, AXES, pairs)


def per_device(queries, key_rows, values, out_weight, out_grad):
    rows, width = queries.shape
    place = [lax.axis_index(axes) for axes in ("x", "core", SEQ[:1], SEQ[:2])]
    place = jnp.stack(place).astype(jnp.int32)

    weight = out_weight.T
    copies = jnp.broadcast_to(weight[None], (SIZES[3],) + weight.shape)
    weight = lax.all_to_all(copies, "y", 0, 0, tiled=True).reshape(-1, width)
    weight = lax.all_gather(weight, SEQ[:3], axis=0, tiled=True)

    grads = [out_grad] + [
        permute(out_grad, lambda across, half, ahead=ahead: (across - ahead, half)) for ahead in (1, 2, 3)
    ]

    local_state = call(state_kernel, shape_of((width, HEAD_DIM), BF16), key_rows, values, name="state")
    prefix, own_grads, other_grads = outside_sum(local_state, 1, False, place, grads)
    numer = call(
        forward_kernel, shape_of((rows, width), F32), queries, key_rows, values, prefix, name="forward"
    )
    numer_grad, local_grad, partial_out = middle(place, own_grads, other_grads, weight, queries, numer)
    mixed = lax.psum_scatter(partial_out, ("x", "core"), scatter_dimension=1, tiled=True)
    query_out, key_part, value_part = call(
        backward_kernel,
        (shape_of((rows, width), BF16),) + (shape_of((rows, width), F32),) * 2,
        queries, key_rows, values, numer_grad, prefix,
        name="backward",
    )
    (suffix,) = outside_sum(local_grad, 2, True, place, before_far=(query_out,))
    key_out, value_out = call(
        suffix_kernel,
        (shape_of((rows, width), BF16),) * 2,
        key_rows, values, suffix, key_part, value_part,
        name="suffix",
    )
    return mixed, query_out, key_out, value_out


def solution(mesh):
    fine = Mesh(mesh.devices.reshape(SIZES), AXES)
    head = AXES[4:]
    rows = P(SEQ, head)
    return jax.shard_map(
        per_device,
        mesh=fine,
        in_specs=(rows, rows, rows, P(head, SEQ), rows),
        out_specs=(rows, rows, rows, rows),
        check_vma=False,
    )
```
